32 devices in a mesh: box: 8 (over y, x, core), term: 4 (over z).
Axes of the slice: x: 2, y: 2, z: 4, core: 2. Of those that a mesh axis runs over, the one named last changes fastest.
Arguments:
- fine_coeffs: bfloat16 [4, 64, 32, 1024], P(None, 'box'), may hold values from -6 to 6
- fine_blocks: bfloat16 [16, 3, 32, 32], replicated, may hold values from -0.625 to 0.625
- coarse_blocks: bfloat16 [16, 3, 32, 32], replicated, may hold values from -0.625 to 0.625
- two_scale: bfloat16 [32, 64], replicated, may hold values from -0.75 to 0.75
- term_exponent: int32 [8], replicated, may hold values from 0 to 15
Outputs:
- applied: float32 [4, 64, 32, 1024], P(None, ('box', 'term'))
The draws below stay inside these ranges and needn't reach their ends.
All inputs are finite; a program needn't handle non-finite values.
Results may differ from the reference program's by a relative error of at most 0.0047.
Values may be sent and summed in bfloat16 or wider, within the bound.
A program may use at most 128 MiB of HBM per device.

```python
import jax
import jax.numpy as jnp
import numpy as np
from jax import lax

K = 32
FUNCS = 4
TERMS = 8
EXPS = 16
G = 2
NPAR = 8
NFINE = 64


def plant(entries, key, smallest, largest):
    shape = entries.shape
    index_at = [jax.random.randint(jax.random.fold_in(key, axis), (), 0, shape[axis]) for axis in range(len(shape))]
    entries = entries.at[tuple(index_at)].set(smallest)
    longest = shape.index(max(shape))
    index_at[longest] = (index_at[longest] + 1) % shape[longest]
    return entries.at[tuple(index_at)].set(largest)


def level_of(stream_key, dims, cuts, smallest, top_value):
    def one(position, parts):
        draws = jax.random.uniform(jax.random.fold_in(jax.random.fold_in(stream_key, 6), position), (parts,), jnp.float32, smallest / len(cuts), top_value / len(cuts))
        return jnp.repeat(jnp.exp(draws), dims[position] // parts).reshape((-1,) + (1,) * (len(dims) - position - 1))

    level = one(*cuts[0])
    for cut in cuts[1:]:
        level = level * one(*cut)
    return level


def noise(key, dims, deviation, bound, cuts=(), held_as=jnp.bfloat16):
    factor_of = level_of(key, dims, cuts, -0.22, 0.18) if cuts else 1.0
    values = jax.random.normal(key, dims, jnp.float32) * deviation * factor_of
    return jnp.minimum(jnp.maximum(values, -bound), bound).astype(held_as)


def setup_inputs(seed: int = 0) -> dict:
    splits = jax.random.split(jax.random.key(seed), 6)
    fine_coeffs = noise(splits[0], (FUNCS, NFINE, K, K * K), 1.0, 6.0, ((1, 8),))
    fine_blocks = noise(splits[1], (EXPS, 3, K, K), (3 * K) ** -0.5, 0.625)
    coarse_blocks = noise(splits[2], (EXPS, 3, K, K), (3 * K) ** -0.5, 0.625)
    two_scale = noise(splits[3], (K, 2 * K), (2 * K) ** -0.5, 0.75)
    term_exponent = plant(jax.random.randint(splits[4], (TERMS,), 0, EXPS), jax.random.fold_in(splits[4], 1), 0, EXPS - 1).astype(jnp.int32)
    return dict(fine_coeffs=fine_coeffs, fine_blocks=fine_blocks, coarse_blocks=coarse_blocks, two_scale=two_scale, term_exponent=term_exponent)


def to_cells(fine_coeffs):
    functions = fine_coeffs.shape[0]
    breadth = fine_coeffs.shape[2]
    cube = fine_coeffs.reshape(functions, NPAR, 2, 2, 2, breadth, breadth, breadth)
    cube = cube.transpose(0, 1, 2, 5, 3, 6, 4, 7)
    return cube.reshape(functions, NPAR, 2 * breadth, 2 * breadth, 2 * breadth)


def from_cells(values):
    functions = values.shape[0]
    breadth = K
    cube = values.reshape(functions, NPAR, 2, breadth, 2, breadth, 2, breadth)
    cube = cube.transpose(0, 1, 2, 4, 6, 3, 5, 7)
    return cube.reshape(functions, NPAR * 8, breadth, breadth * breadth)


def chain_apply(chain, blocks):
    layout = chain.shape
    breadth = layout[-1]
    flattened = chain.reshape(-1, breadth)
    pieces = [jnp.dot(flattened, blocks[offset], preferred_element_type=jnp.float32).reshape(layout) for offset in range(3)]
    return pieces[1] + jnp.roll(pieces[0], 1, axis=-2) + jnp.roll(pieces[2], -1, axis=-2)


def one_pass(values, blocks, along_axis, factor):
    functions = values.shape[0]
    edge = values.shape[2]
    breadth = blocks.shape[-1]
    if along_axis == 4:
        split = (functions, NPAR, edge, edge, factor, breadth)
        order = (0, 2, 3, 1, 4, 5)
    elif along_axis == 3:
        split = (functions, G * G, G, edge, factor, breadth, edge)
        order = (0, 2, 3, 6, 1, 4, 5)
    else:
        split = (functions, G, G * G, factor, breadth, edge, edge)
        order = (0, 2, 5, 6, 1, 3, 4)
    moved = values.reshape(split).transpose(order)
    moved_shape = moved.shape
    chain = moved.reshape(moved_shape[:-3] + (moved_shape[-3] * moved_shape[-2], breadth))
    result = chain_apply(chain, blocks).reshape(moved_shape)
    back = tuple(int(v) for v in np.argsort(np.array(order)))
    return result.transpose(back).reshape(values.shape)


def operate(values, blocks, factor):
    for along_axis in (4, 3, 2):
        values = one_pass(values, blocks, along_axis, factor)
        if along_axis != 2:
            values = values.astype(jnp.bfloat16)
    return values


def reference(fine_coeffs, fine_blocks, coarse_blocks, two_scale, term_exponent):
    fine_cells = to_cells(fine_coeffs)
    parents = jnp.einsum("fpxyz,kz->fpxyk", fine_cells, two_scale, preferred_element_type=jnp.float32).astype(jnp.bfloat16)
    parents = jnp.einsum("fpxyk,jy->fpxjk", parents, two_scale, preferred_element_type=jnp.float32).astype(jnp.bfloat16)
    parents = jnp.einsum("fpxjk,ix->fpijk", parents, two_scale, preferred_element_type=jnp.float32).astype(jnp.bfloat16)
    fine_sum = jnp.zeros(fine_cells.shape, jnp.float32)
    coarse_sum = jnp.zeros(parents.shape, jnp.float32)
    for term_index in range(TERMS):
        chosen = term_exponent[term_index]
        fine_sum = fine_sum + operate(fine_cells, jnp.take(fine_blocks, chosen, axis=0), 2)
        coarse_sum = coarse_sum + operate(parents, jnp.take(coarse_blocks, chosen, axis=0), 1)
    exact_mode = lax.Precision.HIGHEST
    scale_wide = two_scale.astype(jnp.float32)
    spread_out = jnp.einsum("fpijk,kz->fpijz", coarse_sum, scale_wide, precision=exact_mode)
    spread_out = jnp.einsum("fpijz,jy->fpiyz", spread_out, scale_wide, precision=exact_mode)
    spread_out = jnp.einsum("fpiyz,ix->fpxyz", spread_out, scale_wide, precision=exact_mode)
    return from_cells(fine_sum + spread_out)
```

```python
import functools

import jax
import jax.numpy as jnp
from jax import lax
from jax.experimental import pallas as pl
from jax.experimental.pallas import tpu as pltpu
from jax.sharding import PartitionSpec as P

F32 = jnp.float32
BF16 = jnp.bfloat16


def side_count(total):
    return [guess for guess in range(1, 65) if guess * guess * guess == total][0]


def mm(a, b):
    return jnp.dot(a, b, preferred_element_type=F32)


def banded(blocks, own):
    k = blocks.shape[-1]
    columns = []
    for c in range(own):
        columns.append(
            jnp.pad(
                blocks.reshape(blocks.shape[0], 3 * k, k),
                ((0, 0), (c * k, (own - 1 - c) * k), (0, 0)),
            )
        )
    return jnp.concatenate(columns, axis=2)


def level_weights(blocks, own, per):
    terms, _, k, _ = blocks.shape
    band = banded(blocks, own)
    ext = (own + 2) * k
    wx = band.transpose(0, 2, 1).reshape(terms * own * k, ext)
    wy = band.reshape(terms, ext // per, per, own * k).transpose(2, 3, 0, 1)
    wy = wy.reshape(per * own * k, terms * ext // per)
    eye = jnp.eye(per, dtype=blocks.dtype)
    kb = eye[None, None, :, None, :, None] * blocks[:, :, None, :, None, :]
    kb = kb.reshape(terms, 3, per * k, per * k)
    return wx, kb, wy


def spread_blocks(summed, lane_block, k, per):
    rows = summed.shape[0] // per
    kept = summed[:rows]
    for a in range(1, per):
        kept = jnp.where(lane_block == a, summed[a * rows : (a + 1) * rows], kept)
    shift = k
    while shift < per * k:
        kept = kept + pltpu.roll(kept, shift, 1)
        shift *= 2
    return kept


def sweep(load, own, terms, k, per, wx, kb, wy, a_ref, z_ref, out_ref):
    ext = own + 2
    tiles = k // per
    lanes = per * k
    rows = own * k
    lane_block = lax.broadcasted_iota(jnp.int32, (rows, lanes), 1) // k

    def by_y(yb, carry):
        for zb in range(ext):
            a_ref[zb] = mm(wx[...], load(yb, zb)).astype(BF16)

        def by_term(t, carry):
            parts = []
            for zb in range(ext):
                part = a_ref[zb, pl.ds(pl.multiple_of(t * rows, rows), rows), :]
                parts.append(
                    jnp.concatenate(
                        [part[:, i * lanes : (i + 1) * lanes] for i in range(tiles)], axis=0
                    )
                )
            left = jnp.concatenate(parts, axis=1)
            zero = jnp.zeros((lanes, lanes), BF16)
            right = jnp.concatenate(
                [
                    jnp.concatenate(
                        [kb[t, zb - c] if 0 <= zb - c <= 2 else zero for zb in range(ext)], axis=0
                    )
                    for c in range(own)
                ],
                axis=1,
            )
            result = mm(left, right)
            start = pl.multiple_of((t * ext + yb) * tiles * rows, tiles * rows)
            for c in range(own):
                z_ref[c, pl.ds(start, tiles * rows), :] = result[:, c * lanes : (c + 1) * lanes]
            return carry

        return lax.fori_loop(0, terms, by_term, carry)

    lax.fori_loop(0, ext, by_y, 0)

    def by_u(u, carry):
        right = jnp.concatenate(
            [
                z_ref[c, pl.ds(u, terms * ext * tiles, stride=rows), :].astype(BF16)
                for c in range(own)
            ],
            axis=1,
        )
        result = mm(wy[...], right)
        for c in range(own):
            out_ref[c, pl.ds(pl.multiple_of(u * rows, rows), rows), :] = spread_blocks(
                result[:, c * lanes : (c + 1) * lanes], lane_block, k, per
            )
        return carry

    lax.fori_loop(0, rows, by_u, 0)


def two_parts(value, axis):
    high = value.astype(BF16)
    low = (value - high.astype(F32)).astype(BF16)
    return jnp.concatenate([high, low], axis=axis)


def compute(k, per, terms, load_fine, load_coarse, weights, scratch, out_ref):
    wxf, kbf, wyf, wxc, kbc, wyc, wzu, wtu = weights
    a_f, z_f, out_f, a_c, z_c, out_c, d_ref = scratch
    lanes = per * k
    sweep(load_coarse, 1, terms, k, per, wxc, kbc, wyc, a_c, z_c, out_c)
    lane_block = lax.broadcasted_iota(jnp.int32, (k, lanes), 1) // k

    def unfilter(u, carry):
        value = out_c[0, pl.ds(pl.multiple_of(u * k, k), k), :]
        along_z = mm(two_parts(value, 1), wzu[...])
        along_y = mm(wtu[...], two_parts(along_z, 0))
        for c in range(2):
            d_ref[c, pl.ds(pl.multiple_of(u * 2 * k, 2 * k), 2 * k), :] = along_y[
                :, c * lanes : (c + 1) * lanes
            ]
        return carry

    lax.fori_loop(0, k, unfilter, 0)
    sweep(load_fine, 2, terms, k, per, wxf, kbf, wyf, a_f, z_f, out_f)
    wide_block = lax.broadcasted_iota(jnp.int32, (2 * k, lanes), 1) // k
    tiles = k // per
    for cy in range(2):
        for tile in range(tiles):
            for cz in range(2):
                coarse = None
                fine = None
                for a in range(per):
                    v = cy * k + tile * per + a
                    new_c = d_ref[cz, pl.ds(v, k, stride=2 * k), :]
                    new_f = out_f[cz, pl.ds(v, 2 * k, stride=2 * k), :]
                    coarse = new_c if a == 0 else jnp.where(lane_block == a, new_c, coarse)
                    fine = new_f if a == 0 else jnp.where(wide_block == a, new_f, fine)
                total = fine + mm(wtu[...], two_parts(coarse, 0))
                for cx in range(2):
                    out_ref[4 * cx + 2 * cy + cz, :, tile * lanes : (tile + 1) * lanes] = total[
                        cx * k : (cx + 1) * k
                    ].astype(out_ref.dtype)


def kernel(side, k, per, terms, fine_hbm, coarse_hbm, *refs):
    weights = refs[:8]
    out_ref = refs[8]
    scratch = refs[9:16]
    x_f, x_c, sem = refs[16:]
    count = side * side * side
    me = lax.axis_index("box")
    copies = []

    def shift(i):
        return (i + 1) // 2 - 1

    for yb in range(3):
        for zb in range(3):
            for xb in range(3):
                parent = lax.rem(
                    me + 2 * count + (xb - 1) * side * side + (yb - 1) * side + zb - 1, count
                )
                copies.append(
                    pltpu.make_async_copy(
                        coarse_hbm.at[parent], x_c.at[yb, zb, pl.ds(xb * k, k)], sem.at[0]
                    )
                )
    for yb in range(4):
        for zb in range(4):
            for xb in range(4):
                parent = lax.rem(
                    me + 2 * count + shift(xb) * side * side + shift(yb) * side + shift(zb), count
                )
                child = 4 * ((xb + 1) % 2) + 2 * ((yb + 1) % 2) + (zb + 1) % 2
                copies.append(
                    pltpu.make_async_copy(
                        fine_hbm.at[parent, child], x_f.at[yb, zb, pl.ds(xb * k, k)], sem.at[0]
                    )
                )
    for copy in copies:
        copy.start()
    for copy in copies:
        copy.wait()
    compute(
        k,
        per,
        terms,
        lambda yb, zb: x_f[yb, zb],
        lambda yb, zb: x_c[yb, zb],
        weights,
        scratch,
        out_ref,
    )


def prepare(fine_blocks, coarse_blocks, two_scale, exponents, per):
    k = two_scale.shape[0]
    choices = jnp.arange(fine_blocks.shape[0], dtype=jnp.int32)
    selector = (exponents[:, None] == choices[None, :]).astype(BF16)
    fine_terms = jnp.einsum("te,eaij->taij", selector, fine_blocks)
    coarse_terms = jnp.einsum("te,eaij->taij", selector, coarse_blocks)
    fine = level_weights(fine_terms, 2, per)
    coarse = level_weights(coarse_terms, 1, per)
    once = jnp.repeat(two_scale.reshape(k, 2, 1, k), per, axis=2).reshape(k, 2 * per * k)
    once = jnp.pad(once, ((0, (per - 1) * k), (0, 0)))
    wzu = jnp.concatenate([once, once], axis=0)
    wtu = jnp.concatenate([two_scale.T, two_scale.T], axis=1)
    return (*fine, *coarse, wzu, wtu)


def filtered(chosen, two_scale):
    k = two_scale.shape[0]
    cells = chosen.reshape(2, 2, 2, k, k, k)
    scale = two_scale.reshape(k, 2, k)
    parent = jnp.einsum("xyzabe,kze->xyabk", cells, scale, preferred_element_type=F32).astype(BF16)
    parent = jnp.einsum("xyabk,jyb->xajk", parent, scale, preferred_element_type=F32).astype(BF16)
    parent = jnp.einsum("xajk,ixa->ijk", parent, scale, preferred_element_type=F32).astype(BF16)
    return parent.reshape(k, k * k)


def on_device(fine_coeffs, fine_blocks, coarse_blocks, two_scale, term_exponent):
    count = lax.axis_size("box")
    side = side_count(count)
    k = two_scale.shape[0]
    terms = term_exponent.shape[0]
    per = 128 // k
    groups = lax.axis_size("term")
    own = fine_coeffs.shape[0] // groups
    chosen = lax.dynamic_slice_in_dim(fine_coeffs, lax.axis_index("term") * own, own, 0)
    weights = prepare(fine_blocks, coarse_blocks, two_scale, term_exponent, per)
    any_space = pl.BlockSpec(memory_space=pl.ANY)
    vmem = pl.BlockSpec(memory_space=pltpu.VMEM)
    tiles = k // per
    results = []
    for f in range(own):
        parent = filtered(chosen[f], two_scale)
        fine_all = lax.all_gather(chosen[f], "box")
        coarse_all = lax.all_gather(parent, "box")
        results.append(
            pl.pallas_call(
                functools.partial(kernel, side, k, per, terms),
                out_shape=jax.ShapeDtypeStruct((8, k, k * k), F32),
                in_specs=[any_space, any_space] + [vmem] * 8,
                out_specs=vmem,
                scratch_shapes=[
                    pltpu.VMEM((4, terms * 2 * k, k * k), BF16),
                    pltpu.VMEM((2, terms * 4 * tiles * 2 * k, per * k), F32),
                    pltpu.VMEM((2, 4 * k * k, per * k), F32),
                    pltpu.VMEM((3, terms * k, k * k), BF16),
                    pltpu.VMEM((1, terms * 3 * tiles * k, per * k), F32),
                    pltpu.VMEM((1, k * k, per * k), F32),
                    pltpu.VMEM((2, 2 * k * k, per * k), F32),
                    pltpu.VMEM((4, 4, 4 * k, k * k), BF16),
                    pltpu.VMEM((3, 3, 3 * k, k * k), BF16),
                    pltpu.SemaphoreType.DMA((1,)),
                ],
                compiler_params=pltpu.CompilerParams(vmem_limit_bytes=58 * 1024 * 1024),
            )(fine_all, coarse_all, *weights)
        )
    box_rows = jnp.stack(results)
    return lax.all_to_all(box_rows, "term", split_axis=1, concat_axis=0, tiled=True)


def solution(mesh):
    placed = (P(None, "box", None, None), P(), P(), P(), P())
    return jax.shard_map(
        on_device,
        mesh=mesh,
        in_specs=placed,
        out_specs=P(None, ("box", "term"), None, None),
        check_vma=False,
    )
```

```python
import functools

import jax
import jax.numpy as jnp
from jax import lax
from jax.experimental import pallas as pl
from jax.experimental.pallas import tpu as pltpu
from jax.sharding import PartitionSpec as P

F32 = jnp.float32
BF16 = jnp.bfloat16


def side_count(total):
    return [guess for guess in range(1, 65) if guess * guess * guess == total][0]


def mm(a, b):
    return jnp.dot(a, b, preferred_element_type=F32)


def mm_t(a, b):
    return lax.dot_general(a, b, (((0,), (0,)), ((), ())), preferred_element_type=F32)


def iotas(rows, columns):
    shape = (rows, columns)
    return lax.broadcasted_iota(jnp.int32, shape, 0), lax.broadcasted_iota(jnp.int32, shape, 1)


def ones_where(condition):
    return jnp.where(condition, jnp.float32(1), jnp.float32(0)).astype(BF16)


def build_weights(blocks, exponents, own, terms, k, per, stack, wx, kb, wy):
    ext = own + 2
    tiles = k // per
    lanes = per * k
    row, column = iotas(k, lanes)
    tiled = ones_where(column % k == row)
    row, column = iotas(lanes, lanes)
    same = (row // k) == (column // k)
    for t in range(terms):
        for d in range(3):
            block = blocks[exponents[t], d]
            at = (t * 3 + d) * k
            stack[at : at + k, :] = block
            wide = mm(block, tiled)
            tall = jnp.concatenate([wide] * per, axis=0)
            kb[t, d] = jnp.where(same, tall, 0.0).astype(BF16)
    row, column = iotas(3 * k, ext * k)
    for c in range(own):
        place = ones_where(column == c * k + row)
        for t in range(terms):
            part = stack[t * 3 * k : (t + 1) * 3 * k, :]
            at = (t * own + c) * k
            wx[at : at + k, :] = mm_t(part, place).astype(BF16)
    row, column = iotas(terms * 3 * k, terms * ext * tiles)
    term = row // (3 * k)
    within = row - term * (3 * k)
    target = term * (ext * tiles) + within // per
    for a in range(per):
        for c in range(own):
            place = ones_where((column == target + c * tiles) & (within % per == a))
            at = (a * own + c) * k
            wy[at : at + k, :] = mm_t(stack[...], place).astype(BF16)


def spread_blocks(summed, lane_block, k, per):
    rows = summed.shape[0] // per
    kept = summed[:rows]
    for a in range(1, per):
        kept = jnp.where(lane_block == a, summed[a * rows : (a + 1) * rows], kept)
    shift = k
    while shift < per * k:
        kept = kept + pltpu.roll(kept, shift, 1)
        shift *= 2
    return kept


def sweep(load, own, terms, k, per, wx, kb, wy, a_ref, z_ref, out_ref):
    ext = own + 2
    tiles = k // per
    lanes = per * k
    rows = own * k
    lane_block = lax.broadcasted_iota(jnp.int32, (rows, lanes), 1) // k

    def by_y(yb, carry):
        for zb in range(ext):
            a_ref[zb] = mm(wx[...], load(yb, zb)).astype(BF16)

        def by_term(t, carry):
            parts = []
            for zb in range(ext):
                part = a_ref[zb, pl.ds(pl.multiple_of(t * rows, rows), rows), :]
                parts.append(
                    jnp.concatenate(
                        [part[:, i * lanes : (i + 1) * lanes] for i in range(tiles)], axis=0
                    )
                )
            left = jnp.concatenate(parts, axis=1)
            zero = jnp.zeros((lanes, lanes), BF16)
            right = jnp.concatenate(
                [
                    jnp.concatenate(
                        [kb[t, zb - c] if 0 <= zb - c <= 2 else zero for zb in range(ext)], axis=0
                    )
                    for c in range(own)
                ],
                axis=1,
            )
            result = mm(left, right)
            start = pl.multiple_of((t * ext + yb) * tiles * rows, tiles * rows)
            for c in range(own):
                z_ref[c, pl.ds(start, tiles * rows), :] = result[:, c * lanes : (c + 1) * lanes]
            return carry

        return lax.fori_loop(0, terms, by_term, carry, unroll=2)

    lax.fori_loop(0, ext, by_y, 0)

    def by_u(u, carry):
        right = jnp.concatenate(
            [
                z_ref[c, pl.ds(u, terms * ext * tiles, stride=rows), :].astype(BF16)
                for c in range(own)
            ],
            axis=1,
        )
        result = mm(wy[...], right)
        for c in range(own):
            out_ref[c, pl.ds(pl.multiple_of(u * rows, rows), rows), :] = spread_blocks(
                result[:, c * lanes : (c + 1) * lanes], lane_block, k, per
            )
        return carry

    lax.fori_loop(0, rows, by_u, 0, unroll=4)


def two_parts(value, axis):
    high = value.astype(BF16)
    low = (value - high.astype(F32)).astype(BF16)
    return jnp.concatenate([high, low], axis=axis)


def compute(k, per, terms, load_fine, load_coarse, weights, scratch, out_ref):
    wxf, kbf, wyf, wxc, kbc, wyc, wzu, wtu = weights
    a_f, z_f, out_f, a_c, z_c, out_c, d_ref = scratch
    lanes = per * k
    sweep(load_coarse, 1, terms, k, per, wxc, kbc, wyc, a_c, z_c, out_c)
    lane_block = lax.broadcasted_iota(jnp.int32, (k, lanes), 1) // k

    def unfilter(u, carry):
        value = out_c[0, pl.ds(pl.multiple_of(u * k, k), k), :]
        along_z = mm(two_parts(value, 1), wzu[...])
        along_y = mm(wtu[...], two_parts(along_z, 0))
        for c in range(2):
            d_ref[c, pl.ds(pl.multiple_of(u * 2 * k, 2 * k), 2 * k), :] = along_y[
                :, c * lanes : (c + 1) * lanes
            ]
        return carry

    lax.fori_loop(0, k, unfilter, 0, unroll=8)
    sweep(load_fine, 2, terms, k, per, wxf, kbf, wyf, a_f, z_f, out_f)
    wide_block = lax.broadcasted_iota(jnp.int32, (2 * k, lanes), 1) // k
    tiles = k // per
    for cy in range(2):
        for tile in range(tiles):
            for cz in range(2):
                coarse = None
                fine = None
                for a in range(per):
                    v = cy * k + tile * per + a
                    new_c = d_ref[cz, pl.ds(v, k, stride=2 * k), :]
                    new_f = out_f[cz, pl.ds(v, 2 * k, stride=2 * k), :]
                    coarse = new_c if a == 0 else jnp.where(lane_block == a, new_c, coarse)
                    fine = new_f if a == 0 else jnp.where(wide_block == a, new_f, fine)
                total = fine + mm(wtu[...], two_parts(coarse, 0))
                for cx in range(2):
                    out_ref[4 * cx + 2 * cy + cz, :, tile * lanes : (tile + 1) * lanes] = total[
                        cx * k : (cx + 1) * k
                    ].astype(out_ref.dtype)


def kernel(side, k, per, terms, exponents, fine_hbm, coarse_hbm, blocks_f, blocks_c, wzu, wtu, out_ref, *refs):
    scratch = refs[:7]
    x_f, x_c, sem, stack, *built = refs[7:]
    weights = (*built, wzu, wtu)
    count = side * side * side
    me = lax.axis_index("box")
    copies = []

    def shift(i):
        return (i + 1) // 2 - 1

    for yb in range(3):
        for zb in range(3):
            for xb in range(3):
                parent = lax.rem(
                    me + 2 * count + (xb - 1) * side * side + (yb - 1) * side + zb - 1, count
                )
                copies.append(
                    pltpu.make_async_copy(
                        coarse_hbm.at[parent], x_c.at[yb, zb, pl.ds(xb * k, k)], sem.at[0]
                    )
                )
    for yb in range(4):
        for zb in range(4):
            for xb in range(4):
                parent = lax.rem(
                    me + 2 * count + shift(xb) * side * side + shift(yb) * side + shift(zb), count
                )
                child = 4 * ((xb + 1) % 2) + 2 * ((yb + 1) % 2) + (zb + 1) % 2
                copies.append(
                    pltpu.make_async_copy(
                        fine_hbm.at[parent, child], x_f.at[yb, zb, pl.ds(xb * k, k)], sem.at[0]
                    )
                )
    for copy in copies:
        copy.start()
    build_weights(blocks_f, exponents, 2, terms, k, per, stack, *built[:3])
    build_weights(blocks_c, exponents, 1, terms, k, per, stack, *built[3:])
    for copy in copies:
        copy.wait()
    compute(
        k,
        per,
        terms,
        lambda yb, zb: x_f[yb, zb],
        lambda yb, zb: x_c[yb, zb],
        weights,
        scratch,
        out_ref,
    )


def unfilter_weights(two_scale, per):
    k = two_scale.shape[0]
    once = jnp.repeat(two_scale.reshape(k, 2, 1, k), per, axis=2).reshape(k, 2 * per * k)
    once = jnp.pad(once, ((0, (per - 1) * k), (0, 0)))
    wzu = jnp.concatenate([once, once], axis=0)
    wtu = jnp.concatenate([two_scale.T, two_scale.T], axis=1)
    return wzu, wtu


def filtered(chosen, two_scale):
    k = two_scale.shape[0]
    cells = chosen.reshape(2, 2, 2, k, k, k)
    scale = two_scale.reshape(k, 2, k)
    parent = jnp.einsum("xyzabe,kze->xyabk", cells, scale, preferred_element_type=F32).astype(BF16)
    parent = jnp.einsum("xyabk,jyb->xajk", parent, scale, preferred_element_type=F32).astype(BF16)
    parent = jnp.einsum("xajk,ixa->ijk", parent, scale, preferred_element_type=F32).astype(BF16)
    return parent.reshape(k, k * k)


def on_device(fine_coeffs, fine_blocks, coarse_blocks, two_scale, term_exponent):
    count = lax.axis_size("box")
    side = side_count(count)
    k = two_scale.shape[0]
    terms = term_exponent.shape[0]
    per = 128 // k
    groups = lax.axis_size("term")
    own = fine_coeffs.shape[0] // groups
    chosen = lax.dynamic_slice_in_dim(fine_coeffs, lax.axis_index("term") * own, own, 0)
    weights = unfilter_weights(two_scale, per)
    any_space = pl.BlockSpec(memory_space=pl.ANY)
    vmem = pl.BlockSpec(memory_space=pltpu.VMEM)
    tiles = k // per
    results = []
    for f in range(own):
        parent = filtered(chosen[f], two_scale)
        fine_all = lax.all_gather(chosen[f], "box")
        coarse_all = lax.all_gather(parent, "box")
        results.append(
            pl.pallas_call(
                functools.partial(kernel, side, k, per, terms),
                out_shape=jax.ShapeDtypeStruct((8, k, k * k), BF16),
                in_specs=[pl.BlockSpec(memory_space=pltpu.SMEM), any_space, any_space] + [vmem] * 4,
                out_specs=vmem,
                scratch_shapes=[
                    pltpu.VMEM((4, terms * 2 * k, k * k), BF16),
                    pltpu.VMEM((2, terms * 4 * tiles * 2 * k, per * k), F32),
                    pltpu.VMEM((2, 4 * k * k, per * k), F32),
                    pltpu.VMEM((3, terms * k, k * k), BF16),
                    pltpu.VMEM((1, terms * 3 * tiles * k, per * k), F32),
                    pltpu.VMEM((1, k * k, per * k), F32),
                    pltpu.VMEM((2, 2 * k * k, per * k), F32),
                    pltpu.VMEM((4, 4, 4 * k, k * k), BF16),
                    pltpu.VMEM((3, 3, 3 * k, k * k), BF16),
                    pltpu.SemaphoreType.DMA((1,)),
                    pltpu.VMEM((terms * 3 * k, k), BF16),
                    pltpu.VMEM((terms * 2 * k, 4 * k), BF16),
                    pltpu.VMEM((terms, 3, per * k, per * k), BF16),
                    pltpu.VMEM((per * 2 * k, terms * 4 * tiles), BF16),
                    pltpu.VMEM((terms * k, 3 * k), BF16),
                    pltpu.VMEM((terms, 3, per * k, per * k), BF16),
                    pltpu.VMEM((per * k, terms * 3 * tiles), BF16),
                ],
                compiler_params=pltpu.CompilerParams(vmem_limit_bytes=58 * 1024 * 1024),
            )(term_exponent, fine_all, coarse_all, fine_blocks, coarse_blocks, *weights)
        )
    box_rows = jnp.stack(results)
    return lax.all_to_all(box_rows, "term", split_axis=1, concat_axis=0, tiled=True).astype(F32)


def solution(mesh):
    placed = (P(None, "box", None, None), P(), P(), P(), P())
    return jax.shard_map(
        on_device,
        mesh=mesh,
        in_specs=placed,
        out_specs=P(None, ("box", "term"), None, None),
        check_vma=False,
    )
```

```python
import functools

import jax
import jax.numpy as jnp
from jax import lax
from jax.experimental import pallas as pl
from jax.experimental.pallas import tpu as pltpu
from jax.sharding import PartitionSpec as P

F32 = jnp.float32
BF16 = jnp.bfloat16


def side_count(total):
    return [guess for guess in range(1, 65) if guess * guess * guess == total][0]


def mm(a, b):
    return jnp.dot(a, b, preferred_element_type=F32)


def mm_t(a, b):
    return lax.dot_general(a, b, (((0,), (0,)), ((), ())), preferred_element_type=F32)


def iotas(rows, columns):
    shape = (rows, columns)
    return lax.broadcasted_iota(jnp.int32, shape, 0), lax.broadcasted_iota(jnp.int32, shape, 1)


def ones_where(condition):
    return jnp.where(condition, jnp.float32(1), jnp.float32(0)).astype(BF16)


def build_weights(blocks, exponents, own, terms, k, per, stack, wx, kb, wy):
    ext = own + 2
    tiles = k // per
    lanes = per * k
    row, column = iotas(k, lanes)
    tiled = ones_where(column % k == row)
    row, column = iotas(lanes, lanes)
    same = (row // k) == (column // k)
    for t in range(terms):
        for d in range(3):
            block = blocks[exponents[t], d]
            at = (t * 3 + d) * k
            stack[at : at + k, :] = block
            wide = mm(block, tiled)
            tall = jnp.concatenate([wide] * per, axis=0)
            kb[t, d] = jnp.where(same, tall, 0.0).astype(BF16)
    row, column = iotas(3 * k, ext * k)
    for c in range(own):
        place = ones_where(column == c * k + row)
        for t in range(terms):
            part = stack[t * 3 * k : (t + 1) * 3 * k, :]
            at = (t * own + c) * k
            wx[at : at + k, :] = mm_t(part, place).astype(BF16)
    row, column = iotas(terms * 3 * k, terms * ext * tiles)
    term = row // (3 * k)
    within = row - term * (3 * k)
    target = term * (ext * tiles) + within // per
    for a in range(per):
        for c in range(own):
            place = ones_where((column == target + c * tiles) & (within % per == a))
            at = (a * own + c) * k
            wy[at : at + k, :] = mm_t(stack[...], place).astype(BF16)


def spread_blocks(summed, lane_block, k, per):
    rows = summed.shape[0] // per
    kept = summed[:rows]
    for a in range(1, per):
        kept = jnp.where(lane_block == a, summed[a * rows : (a + 1) * rows], kept)
    shift = k
    while shift < per * k:
        kept = kept + pltpu.roll(kept, shift, 1)
        shift *= 2
    return kept


def sweep(load, own, terms, k, per, wx, kb, wy, a_ref, z_ref, out_ref):
    ext = own + 2
    tiles = k // per
    lanes = per * k
    rows = own * k
    lane_block = lax.broadcasted_iota(jnp.int32, (rows, lanes), 1) // k

    def by_y(yb, carry):
        for zb in range(ext):
            a_ref[zb] = mm(wx[...], load(yb, zb)).astype(BF16)

        def by_term(t, carry):
            parts = []
            for zb in range(ext):
                part = a_ref[zb, pl.ds(pl.multiple_of(t * rows, rows), rows), :]
                parts.append(
                    jnp.concatenate(
                        [part[:, i * lanes : (i + 1) * lanes] for i in range(tiles)], axis=0
                    )
                )
            left = jnp.concatenate(parts, axis=1)
            zero = jnp.zeros((lanes, lanes), BF16)
            right = jnp.concatenate(
                [
                    jnp.concatenate(
                        [kb[t, zb - c] if 0 <= zb - c <= 2 else zero for zb in range(ext)], axis=0
                    )
                    for c in range(own)
                ],
                axis=1,
            )
            result = mm(left, right)
            start = pl.multiple_of((t * ext + yb) * tiles * rows, tiles * rows)
            for c in range(own):
                z_ref[c, pl.ds(start, tiles * rows), :] = result[:, c * lanes : (c + 1) * lanes]
            return carry

        return lax.fori_loop(0, terms, by_term, carry, unroll=2)

    lax.fori_loop(0, ext, by_y, 0)

    def by_u(u, carry):
        right = jnp.concatenate(
            [
                z_ref[c, pl.ds(u, terms * ext * tiles, stride=rows), :].astype(BF16)
                for c in range(own)
            ],
            axis=1,
        )
        result = mm(wy[...], right)
        for c in range(own):
            out_ref[c, pl.ds(pl.multiple_of(u * rows, rows), rows), :] = spread_blocks(
                result[:, c * lanes : (c + 1) * lanes], lane_block, k, per
            )
        return carry

    lax.fori_loop(0, rows, by_u, 0, unroll=4)


def two_parts(value, axis):
    high = value.astype(BF16)
    low = (value - high.astype(F32)).astype(BF16)
    return jnp.concatenate([high, low], axis=axis)


def compute(
    k, per, terms, load_fine, load_coarse, weights, scratch, out_ref, ready=lambda: None
):
    wxf, kbf, wyf, wxc, kbc, wyc, wzu, wtu = weights
    a_f, z_f, out_f, a_c, z_c, out_c, d_ref = scratch
    lanes = per * k
    sweep(load_coarse, 1, terms, k, per, wxc, kbc, wyc, a_c, z_c, out_c)
    lane_block = lax.broadcasted_iota(jnp.int32, (k, lanes), 1) // k

    def unfilter(u, carry):
        value = out_c[0, pl.ds(pl.multiple_of(u * k, k), k), :]
        along_z = mm(two_parts(value, 1), wzu[...])
        along_y = mm(wtu[...], two_parts(along_z, 0))
        for c in range(2):
            d_ref[c, pl.ds(pl.multiple_of(u * 2 * k, 2 * k), 2 * k), :] = along_y[
                :, c * lanes : (c + 1) * lanes
            ]
        return carry

    lax.fori_loop(0, k, unfilter, 0, unroll=8)
    ready()
    sweep(load_fine, 2, terms, k, per, wxf, kbf, wyf, a_f, z_f, out_f)
    wide_block = lax.broadcasted_iota(jnp.int32, (2 * k, lanes), 1) // k
    tiles = k // per
    for cy in range(2):
        for tile in range(tiles):
            for cz in range(2):
                coarse = None
                fine = None
                for a in range(per):
                    v = cy * k + tile * per + a
                    new_c = d_ref[cz, pl.ds(v, k, stride=2 * k), :]
                    new_f = out_f[cz, pl.ds(v, 2 * k, stride=2 * k), :]
                    coarse = new_c if a == 0 else jnp.where(lane_block == a, new_c, coarse)
                    fine = new_f if a == 0 else jnp.where(wide_block == a, new_f, fine)
                total = fine + mm(wtu[...], two_parts(coarse, 0))
                for cx in range(2):
                    out_ref[4 * cx + 2 * cy + cz, :, tile * lanes : (tile + 1) * lanes] = total[
                        cx * k : (cx + 1) * k
                    ].astype(out_ref.dtype)


def kernel(side, k, per, terms, exponents, fine_hbm, coarse_hbm, blocks_f, blocks_c, wzu, wtu, out_ref, *refs):
    scratch = refs[:7]
    x_f, x_c, sem, stack, *built = refs[7:]
    weights = (*built, wzu, wtu)
    count = side * side * side
    me = lax.axis_index("box")
    copies = []

    def shift(i):
        return (i + 1) // 2 - 1

    for yb in range(3):
        for zb in range(3):
            for xb in range(3):
                parent = lax.rem(
                    me + 2 * count + (xb - 1) * side * side + (yb - 1) * side + zb - 1, count
                )
                copies.append(
                    pltpu.make_async_copy(
                        coarse_hbm.at[parent], x_c.at[yb, zb, pl.ds(xb * k, k)], sem.at[0]
                    )
                )
    for yb in range(4):
        for zb in range(4):
            for xb in range(4):
                parent = lax.rem(
                    me + 2 * count + shift(xb) * side * side + shift(yb) * side + shift(zb), count
                )
                child = 4 * ((xb + 1) % 2) + 2 * ((yb + 1) % 2) + (zb + 1) % 2
                copies.append(
                    pltpu.make_async_copy(
                        fine_hbm.at[parent, child], x_f.at[yb, zb, pl.ds(xb * k, k)], sem.at[0]
                    )
                )
    for copy in copies:
        copy.start()
    build_weights(blocks_f, exponents, 2, terms, k, per, stack, *built[:3])
    build_weights(blocks_c, exponents, 1, terms, k, per, stack, *built[3:])
    for copy in copies:
        copy.wait()
    compute(
        k,
        per,
        terms,
        lambda yb, zb: x_f[yb, zb],
        lambda yb, zb: x_c[yb, zb],
        weights,
        scratch,
        out_ref,
    )


def two_scale_weights(scale, k, per):
    lanes = per * k
    row, column = iotas(k, lanes)
    tiled = ones_where(column % k == row)
    row, column = iotas(lanes, lanes)
    same = (row // k) == (column // k)
    spread = mm_t(scale, tiled)
    along_z = jnp.concatenate(
        [
            jnp.where(same, jnp.concatenate([spread[c * k : (c + 1) * k]] * per, axis=0), 0.0)
            for c in range(2)
        ],
        axis=0,
    ).astype(BF16)
    row, column = iotas(2 * k, 2 * k // per)
    along_y = jnp.concatenate(
        [mm(scale, ones_where(row == per * column + a)) for a in range(per)], axis=0
    ).astype(BF16)
    row, column = iotas(2 * k, 2 * lanes)
    once = mm(scale, ones_where(row == (column // lanes) * k + column % k)).astype(BF16)
    padded = jnp.concatenate([once, jnp.zeros(((per - 1) * k, 2 * lanes), BF16)], axis=0)
    back_z = jnp.concatenate([padded, padded], axis=0)
    row, column = iotas(k, 2 * k)
    back = mm_t(scale, ones_where(column % k == row)).astype(BF16)
    return along_z, along_y, back_z, back


def filter_own(own, scale, along_z, along_y, k, per, z_ref, y_ref, out):
    tiles = k // per
    lanes = per * k
    for cx in range(2):
        parts = []
        for cz in range(2):
            pieces = []
            for cy in range(2):
                box = own[4 * cx + 2 * cy + cz]
                pieces += [box[:, i * lanes : (i + 1) * lanes] for i in range(tiles)]
            parts.append(jnp.concatenate(pieces, axis=0))
        result = mm(jnp.concatenate(parts, axis=1), along_z[...])
        z_ref[cx * 2 * tiles * k : (cx + 1) * 2 * tiles * k, :] = result
    lane_block = lax.broadcasted_iota(jnp.int32, (k, lanes), 1) // k

    def by_x(x, carry):
        start = (x // k) * (2 * tiles * k) + x % k
        right = z_ref[pl.ds(start, 2 * tiles, stride=k), :].astype(BF16)
        y_ref[pl.ds(pl.multiple_of(x * k, k), k), :] = spread_blocks(
            mm(along_y[...], right), lane_block, k, per
        )
        return carry

    lax.fori_loop(0, 2 * k, by_x, 0, unroll=8)
    wide_block = lax.broadcasted_iota(jnp.int32, (2 * k, lanes), 1) // k
    for tile in range(tiles):
        picked = y_ref[pl.ds(tile * per, 2 * k, stride=k), :]
        for a in range(1, per):
            other = y_ref[pl.ds(tile * per + a, 2 * k, stride=k), :]
            picked = jnp.where(wide_block == a, other, picked)
        out[:, tile * lanes : (tile + 1) * lanes] = mm(scale[...], picked.astype(BF16)).astype(BF16)


def flip(index, mask):
    y, x, c = index // 4, (index // 2) % 2, index % 2
    y = 1 - y if mask & 4 else y
    x = 1 - x if mask & 2 else x
    c = 1 - c if mask & 1 else c
    return 4 * y + 2 * x + c


FINE_ROUTE = {
    (2, 0): (0, 2), (4, 1): (0, 4), (2, 1): (0, 2), (4, 0): (0, 4), (1, 0): (0, 1), (1, 1): (0, 1),
    (6, 0): (2, 4), (6, 1): (4, 2),
    (3, 0): (2, 1), (3, 1): (2, 1), (5, 0): (4, 1), (5, 1): (4, 1), (7, 0): (6, 1), (7, 1): (6, 1),
}
COARSE_ROUTE = {1: (0, 1), 2: (0, 2), 4: (0, 4), 6: (2, 4), 3: (2, 1), 5: (4, 1), 7: (6, 1)}


def fused_kernel(k, per, terms, groups, exponents, fine, blocks_f, blocks_c, scale, out_ref, *refs):
    scratch = refs[:7]
    all_f, all_c, staged, landed = refs[7:11]
    own_sem, send_f, recv_f, send_c, recv_c, send_o, recv_o = refs[11:18]
    stack, back_z, back, along_z, along_y, filter_z, filter_y = refs[18:25]
    built = refs[25:31]
    me = lax.axis_index("box")
    group = lax.axis_index("term")
    own_copy = pltpu.make_async_copy(fine.at[group], all_f.at[me], own_sem.at[0])
    own_copy.start()
    barrier = pltpu.get_barrier_semaphore()
    for mask in (1, 2, 4):
        pl.semaphore_signal(
            barrier, inc=1, device_id={"box": flip(me, mask)}, device_id_type=pl.DeviceIdType.MESH
        )
    for step in range(1, groups):
        pl.semaphore_signal(
            barrier,
            inc=1,
            device_id={"term": lax.rem(group + step, groups)},
            device_id_type=pl.DeviceIdType.MESH,
        )
    pl.semaphore_wait(barrier, 3 + groups - 1)

    def fine_copy(slot, half, source, target):
        ref = all_f.at[flip(me, source), pl.ds(4 * half, 4)]
        return pltpu.make_async_remote_copy(
            src_ref=ref,
            dst_ref=ref,
            send_sem=send_f.at[slot, half],
            recv_sem=recv_f.at[slot, half],
            device_id={"box": flip(me, target)},
            device_id_type=pl.DeviceIdType.MESH,
        )

    def coarse_copy(slot, source, target):
        ref = all_c.at[flip(me, source)]
        return pltpu.make_async_remote_copy(
            src_ref=ref,
            dst_ref=ref,
            send_sem=send_c.at[slot],
            recv_sem=recv_c.at[slot],
            device_id={"box": flip(me, target)},
            device_id_type=pl.DeviceIdType.MESH,
        )

    def push_fine(*keys):
        for key in keys:
            fine_copy(*key, *FINE_ROUTE[key]).start()

    def arrived_fine(*keys):
        for slot, half in keys:
            fine_copy(slot, half, slot, FINE_ROUTE[slot, half][1]).wait_recv()

    def push_coarse(*keys):
        for key in keys:
            coarse_copy(key, *COARSE_ROUTE[key]).start()

    def arrived_coarse(*keys):
        for slot in keys:
            coarse_copy(slot, slot, COARSE_ROUTE[slot][1]).wait_recv()

    own_copy.wait()
    push_fine((2, 0), (4, 1), (2, 1), (4, 0), (1, 0), (1, 1))
    for ref, value in zip((along_z, along_y, back_z, back), two_scale_weights(scale[...], k, per)):
        ref[...] = value
    filter_own(
        all_f.at[me], scale, along_z, along_y, k, per, filter_z, filter_y, all_c.at[me]
    )
    push_coarse(1, 2, 4)
    arrived_fine((2, 0), (4, 1))
    push_fine((6, 0), (6, 1), (3, 0), (5, 1))
    build_weights(blocks_c, exponents, 1, terms, k, per, stack, *built[3:])
    arrived_coarse(2, 4)
    push_coarse(6, 3, 5)
    arrived_fine((2, 1), (4, 0))
    push_fine((3, 1), (5, 0))
    build_weights(blocks_f, exponents, 2, terms, k, per, stack, *built[:3])
    arrived_coarse(6)
    push_coarse(7)
    arrived_fine((6, 0), (6, 1))
    push_fine((7, 0), (7, 1))
    arrived_coarse(1, 3, 5, 7)

    def all_here():
        arrived_fine(
            (1, 0), (1, 1), (3, 0), (3, 1), (5, 0), (5, 1), (7, 0), (7, 1)
        )

    def load_fine(yb, zb):
        parts = []
        for xb in range(4):
            parent = (
                me + 16 + 4 * ((xb + 1) // 2 - 1) + 2 * ((yb + 1) // 2 - 1) + (zb + 1) // 2 - 1
            ) % 8
            child = 4 * ((xb + 1) % 2) + 2 * ((yb + 1) % 2) + (zb + 1) % 2
            parts.append(all_f[parent, child])
        return jnp.concatenate(parts, axis=0)

    def load_coarse(yb, zb):
        parts = [
            all_c[(me + 16 + 4 * (xb - 1) + 2 * (yb - 1) + zb - 1) % 8] for xb in range(3)
        ]
        return jnp.concatenate(parts, axis=0)

    compute(
        k, per, terms, load_fine, load_coarse, (*built, back_z, back), scratch, staged, all_here
    )
    pushes = []
    share = 8 // groups
    for step in range(1, groups):
        target = lax.rem(group + step, groups)
        copy = pltpu.make_async_remote_copy(
            src_ref=staged.at[pl.ds(target * share, share)],
            dst_ref=landed.at[group],
            send_sem=send_o.at[step],
            recv_sem=recv_o.at[step],
            device_id={"term": target},
            device_id_type=pl.DeviceIdType.MESH,
        )
        copy.start()
        pushes.append(copy)
    out_ref[group] = staged[pl.ds(group * share, share)]
    for key, (source, target) in FINE_ROUTE.items():
        fine_copy(*key, source, target).wait_send()
    for key, (source, target) in COARSE_ROUTE.items():
        coarse_copy(key, source, target).wait_send()
    for step in range(1, groups):
        pushes[step - 1].wait()
        origin = lax.rem(group + groups - step, groups)
        out_ref[origin] = landed[origin]


def fused(fine_coeffs, fine_blocks, coarse_blocks, two_scale, exponents, per):
    k = two_scale.shape[0]
    terms = exponents.shape[0]
    groups = lax.axis_size("term")
    tiles = k // per
    lanes = per * k
    vmem = pl.BlockSpec(memory_space=pltpu.VMEM)
    dma = pltpu.SemaphoreType.DMA
    return pl.pallas_call(
        functools.partial(fused_kernel, k, per, terms, groups),
        out_shape=jax.ShapeDtypeStruct((groups, 8 // groups, k, k * k), BF16),
        in_specs=[pl.BlockSpec(memory_space=pltpu.SMEM), pl.BlockSpec(memory_space=pl.ANY)] + [vmem] * 3,
        out_specs=vmem,
        scratch_shapes=pass_scratch(terms, k, per)
        + [
            pltpu.VMEM((8, 8, k, k * k), BF16),
            pltpu.VMEM((8, k, k * k), BF16),
            pltpu.VMEM((8, k, k * k), BF16),
            pltpu.VMEM((groups, 8 // groups, k, k * k), BF16),
            dma((1,)),
            dma((8, 2)),
            dma((8, 2)),
            dma((8,)),
            dma((8,)),
            dma((groups,)),
            dma((groups,)),
            pltpu.VMEM((terms * 3 * k, k), BF16),
            pltpu.VMEM((2 * lanes, 2 * lanes), BF16),
            pltpu.VMEM((2 * k, 2 * k), BF16),
            pltpu.VMEM((2 * lanes, lanes), BF16),
            pltpu.VMEM((lanes, 2 * tiles), BF16),
            pltpu.VMEM((2 * 2 * tiles * k, lanes), F32),
            pltpu.VMEM((2 * k * k, lanes), F32),
        ]
        + weight_scratch(terms, k, per),
        compiler_params=pltpu.CompilerParams(
            vmem_limit_bytes=58 * 1024 * 1024, collective_id=0, has_side_effects=True
        ),
    )(exponents, fine_coeffs, fine_blocks, coarse_blocks, two_scale)


def pass_scratch(terms, k, per):
    tiles = k // per
    return [
        pltpu.VMEM((4, terms * 2 * k, k * k), BF16),
        pltpu.VMEM((2, terms * 4 * tiles * 2 * k, per * k), F32),
        pltpu.VMEM((2, 4 * k * k, per * k), F32),
        pltpu.VMEM((3, terms * k, k * k), BF16),
        pltpu.VMEM((1, terms * 3 * tiles * k, per * k), F32),
        pltpu.VMEM((1, k * k, per * k), F32),
        pltpu.VMEM((2, 2 * k * k, per * k), F32),
    ]


def weight_scratch(terms, k, per):
    tiles = k // per
    return [
        pltpu.VMEM((terms * 2 * k, 4 * k), BF16),
        pltpu.VMEM((terms, 3, per * k, per * k), BF16),
        pltpu.VMEM((per * 2 * k, terms * 4 * tiles), BF16),
        pltpu.VMEM((terms * k, 3 * k), BF16),
        pltpu.VMEM((terms, 3, per * k, per * k), BF16),
        pltpu.VMEM((per * k, terms * 3 * tiles), BF16),
    ]


def unfilter_weights(two_scale, per):
    k = two_scale.shape[0]
    once = jnp.repeat(two_scale.reshape(k, 2, 1, k), per, axis=2).reshape(k, 2 * per * k)
    once = jnp.pad(once, ((0, (per - 1) * k), (0, 0)))
    wzu = jnp.concatenate([once, once], axis=0)
    wtu = jnp.concatenate([two_scale.T, two_scale.T], axis=1)
    return wzu, wtu


def filtered(chosen, two_scale):
    k = two_scale.shape[0]
    cells = chosen.reshape(2, 2, 2, k, k, k)
    scale = two_scale.reshape(k, 2, k)
    parent = jnp.einsum("xyzabe,kze->xyabk", cells, scale, preferred_element_type=F32).astype(BF16)
    parent = jnp.einsum("xyabk,jyb->xajk", parent, scale, preferred_element_type=F32).astype(BF16)
    parent = jnp.einsum("xajk,ixa->ijk", parent, scale, preferred_element_type=F32).astype(BF16)
    return parent.reshape(k, k * k)


def on_device(fine_coeffs, fine_blocks, coarse_blocks, two_scale, term_exponent):
    count = lax.axis_size("box")
    side = side_count(count)
    k = two_scale.shape[0]
    terms = term_exponent.shape[0]
    per = 128 // k
    groups = lax.axis_size("term")
    own = fine_coeffs.shape[0] // groups
    if side == 2 and own == 1 and 8 % groups == 0:
        return fused(
            fine_coeffs, fine_blocks, coarse_blocks, two_scale, term_exponent, per
        ).astype(F32)
    chosen = lax.dynamic_slice_in_dim(fine_coeffs, lax.axis_index("term") * own, own, 0)
    weights = unfilter_weights(two_scale, per)
    any_space = pl.BlockSpec(memory_space=pl.ANY)
    vmem = pl.BlockSpec(memory_space=pltpu.VMEM)
    tiles = k // per
    results = []
    for f in range(own):
        parent = filtered(chosen[f], two_scale)
        fine_all = lax.all_gather(chosen[f], "box")
        coarse_all = lax.all_gather(parent, "box")
        results.append(
            pl.pallas_call(
                functools.partial(kernel, side, k, per, terms),
                out_shape=jax.ShapeDtypeStruct((8, k, k * k), BF16),
                in_specs=[pl.BlockSpec(memory_space=pltpu.SMEM), any_space, any_space] + [vmem] * 4,
                out_specs=vmem,
                scratch_shapes=pass_scratch(terms, k, per)
                + [
                    pltpu.VMEM((4, 4, 4 * k, k * k), BF16),
                    pltpu.VMEM((3, 3, 3 * k, k * k), BF16),
                    pltpu.SemaphoreType.DMA((1,)),
                    pltpu.VMEM((terms * 3 * k, k), BF16),
                ]
                + weight_scratch(terms, k, per),
                compiler_params=pltpu.CompilerParams(vmem_limit_bytes=58 * 1024 * 1024),
            )(term_exponent, fine_all, coarse_all, fine_blocks, coarse_blocks, *weights)
        )
    box_rows = jnp.stack(results)
    return lax.all_to_all(box_rows, "term", split_axis=1, concat_axis=0, tiled=True).astype(F32)


def solution(mesh):
    placed = (P(None, "box", None, None), P(), P(), P(), P())
    return jax.shard_map(
        on_device,
        mesh=mesh,
        in_specs=placed,
        out_specs=P(None, ("box", "term"), None, None),
        check_vma=False,
    )
```

```python
import functools

import jax
import jax.numpy as jnp
from jax import lax
from jax.experimental import pallas as pl
from jax.experimental.pallas import tpu as pltpu
from jax.sharding import PartitionSpec as P

F32 = jnp.float32
BF16 = jnp.bfloat16


def side_count(total):
    return [guess for guess in range(1, 65) if guess * guess * guess == total][0]


def mm(a, b):
    return jnp.dot(a, b, preferred_element_type=F32)


def mm_t(a, b):
    return lax.dot_general(a, b, (((0,), (0,)), ((), ())), preferred_element_type=F32)


def iotas(rows, columns):
    shape = (rows, columns)
    return lax.broadcasted_iota(jnp.int32, shape, 0), lax.broadcasted_iota(jnp.int32, shape, 1)


def ones_where(condition):
    return jnp.where(condition, jnp.float32(1), jnp.float32(0)).astype(BF16)


def build_weights(blocks, exponents, own, terms, k, per, stack, wx, kb, wy):
    ext = own + 2
    tiles = k // per
    lanes = per * k
    row, column = iotas(k, lanes)
    tiled = ones_where(column % k == row)
    row, column = iotas(lanes, lanes)
    same = (row // k) == (column // k)
    for t in range(terms):
        for d in range(3):
            block = blocks[exponents[t], d]
            at = (t * 3 + d) * k
            stack[at : at + k, :] = block
            wide = mm(block, tiled)
            tall = jnp.concatenate([wide] * per, axis=0)
            kb[t, d] = jnp.where(same, tall, 0.0).astype(BF16)
    row, column = iotas(3 * k, ext * k)
    for c in range(own):
        place = ones_where(column == c * k + row)
        for t in range(terms):
            part = stack[t * 3 * k : (t + 1) * 3 * k, :]
            at = (t * own + c) * k
            wx[at : at + k, :] = mm_t(part, place).astype(BF16)
    row, column = iotas(terms * 3 * k, terms * ext * tiles)
    term = row // (3 * k)
    within = row - term * (3 * k)
    target = term * (ext * tiles) + within // per
    for a in range(per):
        for c in range(own):
            place = ones_where((column == target + c * tiles) & (within % per == a))
            at = (a * own + c) * k
            wy[at : at + k, :] = mm_t(stack[...], place).astype(BF16)


def spread_blocks(summed, lane_block, k, per):
    rows = summed.shape[0] // per
    kept = summed[:rows]
    for a in range(1, per):
        kept = jnp.where(lane_block == a, summed[a * rows : (a + 1) * rows], kept)
    shift = k
    while shift < per * k:
        kept = kept + pltpu.roll(kept, shift, 1)
        shift *= 2
    return kept


def sweep(load, own, terms, k, per, wx, kb, wy, a_ref, z_ref, out_ref):
    ext = own + 2
    tiles = k // per
    lanes = per * k
    rows = own * k
    lane_block = lax.broadcasted_iota(jnp.int32, (rows, lanes), 1) // k

    def by_y(yb, carry):
        for zb in range(ext):
            a_ref[zb] = mm(wx[...], load(yb, zb)).astype(BF16)

        def by_term(t, carry):
            parts = []
            for zb in range(ext):
                part = a_ref[zb, pl.ds(pl.multiple_of(t * rows, rows), rows), :]
                parts.append(
                    jnp.concatenate(
                        [part[:, i * lanes : (i + 1) * lanes] for i in range(tiles)], axis=0
                    )
                )
            left = jnp.concatenate(parts, axis=1)
            zero = jnp.zeros((lanes, lanes), BF16)
            right = jnp.concatenate(
                [
                    jnp.concatenate(
                        [kb[t, zb - c] if 0 <= zb - c <= 2 else zero for zb in range(ext)], axis=0
                    )
                    for c in range(own)
                ],
                axis=1,
            )
            result = mm(left, right)
            start = pl.multiple_of((t * ext + yb) * tiles * rows, tiles * rows)
            for c in range(own):
                z_ref[c, pl.ds(start, tiles * rows), :] = result[:, c * lanes : (c + 1) * lanes]
            return carry

        return lax.fori_loop(0, terms, by_term, carry, unroll=4)

    lax.fori_loop(0, ext, by_y, 0)

    def by_u(u, carry):
        right = jnp.concatenate(
            [
                z_ref[c, pl.ds(u, terms * ext * tiles, stride=rows), :].astype(BF16)
                for c in range(own)
            ],
            axis=1,
        )
        result = mm(wy[...], right)
        for c in range(own):
            out_ref[c, pl.ds(pl.multiple_of(u * rows, rows), rows), :] = spread_blocks(
                result[:, c * lanes : (c + 1) * lanes], lane_block, k, per
            )
        return carry

    lax.fori_loop(0, rows, by_u, 0, unroll=8)


def two_parts(value, axis):
    high = value.astype(BF16)
    low = (value - high.astype(F32)).astype(BF16)
    return jnp.concatenate([high, low], axis=axis)


def compute(
    k, per, terms, load_fine, load_coarse, weights, scratch, out_ref, relay=lambda: None, ready=lambda: None,
    done=lambda cy: None,
):
    wxf, kbf, wyf, wxc, kbc, wyc, wzu, wtu = weights
    a_f, z_f, out_f, a_c, z_c, out_c, d_ref = scratch
    lanes = per * k
    sweep(load_coarse, 1, terms, k, per, wxc, kbc, wyc, a_c, z_c, out_c)
    relay()
    lane_block = lax.broadcasted_iota(jnp.int32, (k, lanes), 1) // k

    def unfilter(u, carry):
        value = out_c[0, pl.ds(pl.multiple_of(u * k, k), k), :]
        along_z = mm(two_parts(value, 1), wzu[...])
        along_y = mm(wtu[...], two_parts(along_z, 0))
        for c in range(2):
            d_ref[c, pl.ds(pl.multiple_of(u * 2 * k, 2 * k), 2 * k), :] = along_y[
                :, c * lanes : (c + 1) * lanes
            ]
        return carry

    lax.fori_loop(0, k, unfilter, 0, unroll=8)
    ready()
    sweep(load_fine, 2, terms, k, per, wxf, kbf, wyf, a_f, z_f, out_f)
    wide_block = lax.broadcasted_iota(jnp.int32, (2 * k, lanes), 1) // k
    tiles = k // per
    for cy in range(2):
        for tile in range(tiles):
            for cz in range(2):
                coarse = None
                fine = None
                for a in range(per):
                    v = cy * k + tile * per + a
                    new_c = d_ref[cz, pl.ds(v, k, stride=2 * k), :]
                    new_f = out_f[cz, pl.ds(v, 2 * k, stride=2 * k), :]
                    coarse = new_c if a == 0 else jnp.where(lane_block == a, new_c, coarse)
                    fine = new_f if a == 0 else jnp.where(wide_block == a, new_f, fine)
                total = fine + mm(wtu[...], two_parts(coarse, 0))
                for cx in range(2):
                    out_ref[4 * cx + 2 * cy + cz, :, tile * lanes : (tile + 1) * lanes] = total[
                        cx * k : (cx + 1) * k
                    ].astype(out_ref.dtype)
        done(cy)


def kernel(side, k, per, terms, exponents, fine_hbm, coarse_hbm, blocks_f, blocks_c, wzu, wtu, out_ref, *refs):
    scratch = refs[:7]
    x_f, x_c, sem, stack, *built = refs[7:]
    weights = (*built, wzu, wtu)
    count = side * side * side
    me = lax.axis_index("box")
    copies = []

    def shift(i):
        return (i + 1) // 2 - 1

    for yb in range(3):
        for zb in range(3):
            for xb in range(3):
                parent = lax.rem(
                    me + 2 * count + (xb - 1) * side * side + (yb - 1) * side + zb - 1, count
                )
                copies.append(
                    pltpu.make_async_copy(
                        coarse_hbm.at[parent], x_c.at[yb, zb, pl.ds(xb * k, k)], sem.at[0]
                    )
                )
    for yb in range(4):
        for zb in range(4):
            for xb in range(4):
                parent = lax.rem(
                    me + 2 * count + shift(xb) * side * side + shift(yb) * side + shift(zb), count
                )
                child = 4 * ((xb + 1) % 2) + 2 * ((yb + 1) % 2) + (zb + 1) % 2
                copies.append(
                    pltpu.make_async_copy(
                        fine_hbm.at[parent, child], x_f.at[yb, zb, pl.ds(xb * k, k)], sem.at[0]
                    )
                )
    for copy in copies:
        copy.start()
    build_weights(blocks_f, exponents, 2, terms, k, per, stack, *built[:3])
    build_weights(blocks_c, exponents, 1, terms, k, per, stack, *built[3:])
    for copy in copies:
        copy.wait()
    compute(
        k,
        per,
        terms,
        lambda yb, zb: x_f[yb, zb],
        lambda yb, zb: x_c[yb, zb],
        weights,
        scratch,
        out_ref,
    )


def two_scale_weights(scale, k, per):
    lanes = per * k
    row, column = iotas(k, lanes)
    tiled = ones_where(column % k == row)
    row, column = iotas(lanes, lanes)
    same = (row // k) == (column // k)
    spread = mm_t(scale, tiled)
    along_z = jnp.concatenate(
        [
            jnp.where(same, jnp.concatenate([spread[c * k : (c + 1) * k]] * per, axis=0), 0.0)
            for c in range(2)
        ],
        axis=0,
    ).astype(BF16)
    row, column = iotas(2 * k, 2 * k // per)
    along_y = jnp.concatenate(
        [mm(scale, ones_where(row == per * column + a)) for a in range(per)], axis=0
    ).astype(BF16)
    row, column = iotas(2 * k, 2 * lanes)
    once = mm(scale, ones_where(row == (column // lanes) * k + column % k)).astype(BF16)
    padded = jnp.concatenate([once, jnp.zeros(((per - 1) * k, 2 * lanes), BF16)], axis=0)
    back_z = jnp.concatenate([padded, padded], axis=0)
    row, column = iotas(k, 2 * k)
    back = mm_t(scale, ones_where(column % k == row)).astype(BF16)
    return along_z, along_y, back_z, back


def filter_own(own, scale, along_z, along_y, k, per, z_ref, y_ref, out):
    tiles = k // per
    lanes = per * k
    for cx in range(2):
        parts = []
        for cz in range(2):
            pieces = []
            for cy in range(2):
                box = own[4 * cx + 2 * cy + cz]
                pieces += [box[:, i * lanes : (i + 1) * lanes] for i in range(tiles)]
            parts.append(jnp.concatenate(pieces, axis=0))
        result = mm(jnp.concatenate(parts, axis=1), along_z[...])
        z_ref[cx * 2 * tiles * k : (cx + 1) * 2 * tiles * k, :] = result
    lane_block = lax.broadcasted_iota(jnp.int32, (k, lanes), 1) // k

    def by_x(x, carry):
        start = (x // k) * (2 * tiles * k) + x % k
        right = z_ref[pl.ds(start, 2 * tiles, stride=k), :].astype(BF16)
        y_ref[pl.ds(pl.multiple_of(x * k, k), k), :] = spread_blocks(
            mm(along_y[...], right), lane_block, k, per
        )
        return carry

    lax.fori_loop(0, 2 * k, by_x, 0, unroll=8)
    wide_block = lax.broadcasted_iota(jnp.int32, (2 * k, lanes), 1) // k
    for tile in range(tiles):
        picked = y_ref[pl.ds(tile * per, 2 * k, stride=k), :]
        for a in range(1, per):
            other = y_ref[pl.ds(tile * per + a, 2 * k, stride=k), :]
            picked = jnp.where(wide_block == a, other, picked)
        out[:, tile * lanes : (tile + 1) * lanes] = mm(scale[...], picked.astype(BF16)).astype(BF16)


def flip(index, mask):
    y, x, c = index // 4, (index // 2) % 2, index % 2
    y = 1 - y if mask & 4 else y
    x = 1 - x if mask & 2 else x
    c = 1 - c if mask & 1 else c
    return 4 * y + 2 * x + c


FINE_ROUTE = {
    (2, 0): (0, 2), (4, 1): (0, 4), (2, 1): (0, 2), (4, 0): (0, 4), (1, 0): (0, 1), (1, 1): (0, 1),
    (6, 0): (2, 4), (6, 1): (4, 2),
    (3, 0): (2, 1), (3, 1): (2, 1), (5, 0): (4, 1), (5, 1): (4, 1), (7, 0): (6, 1), (7, 1): (6, 1),
}
COARSE_ROUTE = {1: (0, 1), 2: (0, 2), 4: (0, 4), 6: (2, 4), 3: (2, 1), 5: (4, 1), 7: (6, 1)}


def fused_kernel(k, per, terms, groups, exponents, fine, blocks_f, blocks_c, scale, out_ref, *refs):
    scratch = refs[:7]
    all_f, all_c, staged, landed = refs[7:11]
    own_sem, send_f, recv_f, send_c, recv_c, send_o, recv_o = refs[11:18]
    stack, back_z, back, along_z, along_y, filter_z, filter_y = refs[18:25]
    built = refs[25:31]
    me = lax.axis_index("box")
    group = lax.axis_index("term")
    own_copy = pltpu.make_async_copy(fine.at[group], all_f.at[me], own_sem.at[0])
    own_copy.start()
    barrier = pltpu.get_barrier_semaphore()
    for mask in (1, 2, 4):
        pl.semaphore_signal(
            barrier, inc=1, device_id={"box": flip(me, mask)}, device_id_type=pl.DeviceIdType.MESH
        )
    for step in range(1, groups):
        pl.semaphore_signal(
            barrier,
            inc=1,
            device_id={"term": lax.rem(group + step, groups)},
            device_id_type=pl.DeviceIdType.MESH,
        )
    pl.semaphore_wait(barrier, 3 + groups - 1)

    def fine_copy(slot, half, source, target):
        ref = all_f.at[flip(me, source), pl.ds(4 * half, 4)]
        return pltpu.make_async_remote_copy(
            src_ref=ref,
            dst_ref=ref,
            send_sem=send_f.at[slot, half],
            recv_sem=recv_f.at[slot, half],
            device_id={"box": flip(me, target)},
            device_id_type=pl.DeviceIdType.MESH,
        )

    def coarse_copy(slot, source, target):
        ref = all_c.at[flip(me, source)]
        return pltpu.make_async_remote_copy(
            src_ref=ref,
            dst_ref=ref,
            send_sem=send_c.at[slot],
            recv_sem=recv_c.at[slot],
            device_id={"box": flip(me, target)},
            device_id_type=pl.DeviceIdType.MESH,
        )

    def push_fine(*keys):
        for key in keys:
            fine_copy(*key, *FINE_ROUTE[key]).start()

    def arrived_fine(*keys):
        for slot, half in keys:
            fine_copy(slot, half, slot, FINE_ROUTE[slot, half][1]).wait_recv()

    def push_coarse(*keys):
        for key in keys:
            coarse_copy(key, *COARSE_ROUTE[key]).start()

    def arrived_coarse(*keys):
        for slot in keys:
            coarse_copy(slot, slot, COARSE_ROUTE[slot][1]).wait_recv()

    own_copy.wait()
    push_fine((2, 0), (4, 1), (2, 1), (4, 0), (1, 0), (1, 1))
    for ref, value in zip((along_z, along_y, back_z, back), two_scale_weights(scale[...], k, per)):
        ref[...] = value
    filter_own(
        all_f.at[me], scale, along_z, along_y, k, per, filter_z, filter_y, all_c.at[me]
    )
    push_coarse(1, 2, 4)
    arrived_fine((2, 0), (4, 1))
    push_fine((6, 0), (6, 1), (3, 0), (5, 1))
    build_weights(blocks_c, exponents, 1, terms, k, per, stack, *built[3:])
    arrived_coarse(2, 4)
    push_coarse(6, 3, 5)
    arrived_fine((2, 1), (4, 0))
    push_fine((3, 1), (5, 0))
    build_weights(blocks_f, exponents, 2, terms, k, per, stack, *built[:3])
    arrived_coarse(6)
    push_coarse(7)
    arrived_coarse(1, 3, 5, 7)

    def relay_last():
        arrived_fine((6, 0), (6, 1))
        push_fine((7, 0), (7, 1))

    def all_here():
        arrived_fine(
            (1, 0), (1, 1), (3, 0), (3, 1), (5, 0), (5, 1), (7, 0), (7, 1)
        )

    def load_fine(yb, zb):
        parts = []
        for xb in range(4):
            parent = (
                me + 16 + 4 * ((xb + 1) // 2 - 1) + 2 * ((yb + 1) // 2 - 1) + (zb + 1) // 2 - 1
            ) % 8
            child = 4 * ((xb + 1) % 2) + 2 * ((yb + 1) % 2) + (zb + 1) % 2
            parts.append(all_f[parent, child])
        return jnp.concatenate(parts, axis=0)

    def load_coarse(yb, zb):
        parts = [
            all_c[(me + 16 + 4 * (xb - 1) + 2 * (yb - 1) + zb - 1) % 8] for xb in range(3)
        ]
        return jnp.concatenate(parts, axis=0)

    share = 8 // groups

    def push_result(target):
        step = lax.rem(target - group + groups, groups)
        return pltpu.make_async_remote_copy(
            src_ref=staged.at[pl.ds(target * share, share)],
            dst_ref=landed.at[group],
            send_sem=send_o.at[step],
            recv_sem=recv_o.at[step],
            device_id={"term": target},
            device_id_type=pl.DeviceIdType.MESH,
        )

    def done(cy):
        ready = [cy, 2 + cy] if share == 2 else range(groups * cy)
        for target in ready:
            pl.when(group != target)(lambda target=target: push_result(target).start())

    compute(
        k, per, terms, load_fine, load_coarse, (*built, back_z, back), scratch, staged,
        relay_last, all_here, done,
    )
    out_ref[group] = staged[pl.ds(group * share, share)]
    for key, (source, target) in FINE_ROUTE.items():
        fine_copy(*key, source, target).wait_send()
    for key, (source, target) in COARSE_ROUTE.items():
        coarse_copy(key, source, target).wait_send()
    for step in range(1, groups):
        push_result(lax.rem(group + step, groups)).wait()
        origin = lax.rem(group + groups - step, groups)
        out_ref[origin] = landed[origin]


def fused(fine_coeffs, fine_blocks, coarse_blocks, two_scale, exponents, per):
    k = two_scale.shape[0]
    terms = exponents.shape[0]
    groups = lax.axis_size("term")
    tiles = k // per
    lanes = per * k
    vmem = pl.BlockSpec(memory_space=pltpu.VMEM)
    dma = pltpu.SemaphoreType.DMA
    return pl.pallas_call(
        functools.partial(fused_kernel, k, per, terms, groups),
        out_shape=jax.ShapeDtypeStruct((groups, 8 // groups, k, k * k), BF16),
        in_specs=[pl.BlockSpec(memory_space=pltpu.SMEM), pl.BlockSpec(memory_space=pl.ANY)] + [vmem] * 3,
        out_specs=vmem,
        scratch_shapes=pass_scratch(terms, k, per)
        + [
            pltpu.VMEM((8, 8, k, k * k), BF16),
            pltpu.VMEM((8, k, k * k), BF16),
            pltpu.VMEM((8, k, k * k), BF16),
            pltpu.VMEM((groups, 8 // groups, k, k * k), BF16),
            dma((1,)),
            dma((8, 2)),
            dma((8, 2)),
            dma((8,)),
            dma((8,)),
            dma((groups,)),
            dma((groups,)),
            pltpu.VMEM((terms * 3 * k, k), BF16),
            pltpu.VMEM((2 * lanes, 2 * lanes), BF16),
            pltpu.VMEM((2 * k, 2 * k), BF16),
            pltpu.VMEM((2 * lanes, lanes), BF16),
            pltpu.VMEM((lanes, 2 * tiles), BF16),
            pltpu.VMEM((2 * 2 * tiles * k, lanes), F32),
            pltpu.VMEM((2 * k * k, lanes), F32),
        ]
        + weight_scratch(terms, k, per),
        compiler_params=pltpu.CompilerParams(
            vmem_limit_bytes=58 * 1024 * 1024, collective_id=0, has_side_effects=True
        ),
    )(exponents, fine_coeffs, fine_blocks, coarse_blocks, two_scale)


def pass_scratch(terms, k, per):
    tiles = k // per
    return [
        pltpu.VMEM((4, terms * 2 * k, k * k), BF16),
        pltpu.VMEM((2, terms * 4 * tiles * 2 * k, per * k), F32),
        pltpu.VMEM((2, 4 * k * k, per * k), F32),
        pltpu.VMEM((3, terms * k, k * k), BF16),
        pltpu.VMEM((1, terms * 3 * tiles * k, per * k), F32),
        pltpu.VMEM((1, k * k, per * k), F32),
        pltpu.VMEM((2, 2 * k * k, per * k), F32),
    ]


def weight_scratch(terms, k, per):
    tiles = k // per
    return [
        pltpu.VMEM((terms * 2 * k, 4 * k), BF16),
        pltpu.VMEM((terms, 3, per * k, per * k), BF16),
        pltpu.VMEM((per * 2 * k, terms * 4 * tiles), BF16),
        pltpu.VMEM((terms * k, 3 * k), BF16),
        pltpu.VMEM((terms, 3, per * k, per * k), BF16),
        pltpu.VMEM((per * k, terms * 3 * tiles), BF16),
    ]


def unfilter_weights(two_scale, per):
    k = two_scale.shape[0]
    once = jnp.repeat(two_scale.reshape(k, 2, 1, k), per, axis=2).reshape(k, 2 * per * k)
    once = jnp.pad(once, ((0, (per - 1) * k), (0, 0)))
    wzu = jnp.concatenate([once, once], axis=0)
    wtu = jnp.concatenate([two_scale.T, two_scale.T], axis=1)
    return wzu, wtu


def filtered(chosen, two_scale):
    k = two_scale.shape[0]
    cells = chosen.reshape(2, 2, 2, k, k, k)
    scale = two_scale.reshape(k, 2, k)
    parent = jnp.einsum("xyzabe,kze->xyabk", cells, scale, preferred_element_type=F32).astype(BF16)
    parent = jnp.einsum("xyabk,jyb->xajk", parent, scale, preferred_element_type=F32).astype(BF16)
    parent = jnp.einsum("xajk,ixa->ijk", parent, scale, preferred_element_type=F32).astype(BF16)
    return parent.reshape(k, k * k)


def on_device(fine_coeffs, fine_blocks, coarse_blocks, two_scale, term_exponent):
    count = lax.axis_size("box")
    side = side_count(count)
    k = two_scale.shape[0]
    terms = term_exponent.shape[0]
    per = 128 // k
    groups = lax.axis_size("term")
    own = fine_coeffs.shape[0] // groups
    if side == 2 and own == 1 and 8 % groups == 0:
        return fused(
            fine_coeffs, fine_blocks, coarse_blocks, two_scale, term_exponent, per
        ).astype(F32)
    chosen = lax.dynamic_slice_in_dim(fine_coeffs, lax.axis_index("term") * own, own, 0)
    weights = unfilter_weights(two_scale, per)
    any_space = pl.BlockSpec(memory_space=pl.ANY)
    vmem = pl.BlockSpec(memory_space=pltpu.VMEM)
    tiles = k // per
    results = []
    for f in range(own):
        parent = filtered(chosen[f], two_scale)
        fine_all = lax.all_gather(chosen[f], "box")
        coarse_all = lax.all_gather(parent, "box")
        results.append(
            pl.pallas_call(
                functools.partial(kernel, side, k, per, terms),
                out_shape=jax.ShapeDtypeStruct((8, k, k * k), BF16),
                in_specs=[pl.BlockSpec(memory_space=pltpu.SMEM), any_space, any_space] + [vmem] * 4,
                out_specs=vmem,
                scratch_shapes=pass_scratch(terms, k, per)
                + [
                    pltpu.VMEM((4, 4, 4 * k, k * k), BF16),
                    pltpu.VMEM((3, 3, 3 * k, k * k), BF16),
                    pltpu.SemaphoreType.DMA((1,)),
                    pltpu.VMEM((terms * 3 * k, k), BF16),
                ]
                + weight_scratch(terms, k, per),
                compiler_params=pltpu.CompilerParams(vmem_limit_bytes=58 * 1024 * 1024),
            )(term_exponent, fine_all, coarse_all, fine_blocks, coarse_blocks, *weights)
        )
    box_rows = jnp.stack(results)
    return lax.all_to_all(box_rows, "term", split_axis=1, concat_axis=0, tiled=True).astype(F32)


def solution(mesh):
    placed = (P(None, "box", None, None), P(), P(), P(), P())
    return jax.shard_map(
        on_device,
        mesh=mesh,
        in_specs=placed,
        out_specs=P(None, ("box", "term"), None, None),
        check_vma=False,
    )
```
